256 devices in a mesh: rep: 4 (over y), ep: 64 (over z, x, core).
Axes of the slice: x: 4, y: 4, z: 8, core: 2. Of those that a mesh axis runs over, the one named last changes fastest.
Arguments:
- tokens: bfloat16 [4096, 3584], P(('rep', 'ep')), may hold values from -6 to 6
- chosen_expert_index: int32 [4096, 8], P(('rep', 'ep')), may hold values from 0 to 127, all different within a row; in each aligned block of 16 rows (0 to 15, 16 to 31, ...) at most 2 rows name the same one
- expert_mixing_weight: bfloat16 [4096, 8], P(('rep', 'ep')), may hold values from 0.099609375 to 0.59765625
- row_adapter_index: int32 [4096], P(('rep', 'ep')), may hold values from 0 to 7
- gate_weight: bfloat16 [128, 3584, 1024], P('ep', None, 'rep'), may hold values from -0.09375 to 0.09375
- up_weight: bfloat16 [128, 3584, 1024], P('ep', None, 'rep'), may hold values from -0.09375 to 0.09375
- down_weight: bfloat16 [128, 1024, 3584], P('ep', None, 'rep'), may hold values from -0.1875 to 0.1875
- adapter_down_factor: bfloat16 [3584, 128], replicated, may hold values from -0.09375 to 0.09375
- adapter_up_factor: bfloat16 [128, 1024], P(None, 'rep'), may hold values from -0.75 to 0.75
Outputs:
- mixed: bfloat16 [4096, 3584], P(('rep', 'ep'))
The draws below stay inside these ranges and needn't reach their ends.
Inputs may be any that keep to these rules, and one draw needn't show every extreme that they name: `chosen_expert_index`: each row names 8 different experts. Among the rows of one device no expert is named more than 2 times, a bound that some block reaches.
All inputs are finite; a program needn't handle non-finite values.
Results may differ from the reference program's by a relative error of at most 0.0059.
Values may be sent and summed in bfloat16 or wider, within the bound.
No kernel may reach another device: no remote copies, remote signals or barrier semaphores. Data moves between devices by JAX's collectives and lax.ppermute only.
A program may use at most 128 MiB of HBM per device.

```python
import math
import jax
import jax.numpy as jnp
import numpy as np
from jax import lax

MODEL_WIDTH = 3584
HIDDEN_WIDTH = 1024
TOP = 8
ADAPTER_RANK = 16
ADAPTER_COUNT = 8
ROWS_DEV = 16
EXPERTS = 128
ROWS = 4096
CAP = 2
N_REP = 4
N_EP = 64


def touch_ends(result, own_key, low, top_value):
    spot = [jax.random.randint(jax.random.fold_in(own_key, axis), (), 0, length) for axis, length in enumerate(result.shape)]
    widest = result.shape.index(max(result.shape))
    next_to = spot[:widest] + [(spot[widest] + 1) % result.shape[widest]] + spot[widest + 1:]
    return result.at[tuple(spot)].set(low).at[tuple(next_to)].set(top_value)


def shard_levels(own_key, shape, split, smallest, largest):
    factor_of = 1.0
    for axis_at, parts in split:
        draws = jax.random.uniform(jax.random.fold_in(jax.random.fold_in(own_key, 6), axis_at), (parts,), jnp.float32, smallest / len(split), largest / len(split))
        factor_of = factor_of * jnp.repeat(jnp.exp(draws), shape[axis_at] // parts).reshape((-1,) + (1,) * (len(shape) - 1 - axis_at))
    return factor_of


def deal_out(key, own, number, rows, amount, top, limit, lean):
    ranking = jax.random.permutation(key, amount)
    heavy_load, common = load_shares(amount, rows * top, limit, lean, True), load_shares(amount, rows * top, limit, lean, False)
    places = jnp.arange(amount)

    def named(lengths, rotation):
        used = int((lengths > 0).sum())
        fixed = max(1, used // 4)
        passed = fixed + (places - fixed + rotation * (used - fixed)) % max(1, amount - fixed)
        return jnp.zeros((amount,), jnp.int32).at[ranking[jnp.where(places < fixed, places, passed)]].set(jnp.asarray(lengths, jnp.int32))

    lengths = jnp.where(number % 4 == 0, named(heavy_load, number // 4), named(common, number - number // 4 - 1))
    mixed = jax.random.permutation(jax.random.fold_in(own, 3), amount)
    donor, sink = mixed[0:amount // 2 * 2:2], mixed[1:amount // 2 * 2:2]
    margin = jnp.minimum(lengths[donor] - 1, limit - lengths[sink]) // 2
    margin = jnp.where((donor == ranking[0]) | (sink == ranking[0]) | (lengths[sink] == 0), 0, jnp.maximum(margin, 0))
    passed = jax.random.randint(jax.random.fold_in(own, 4), (amount // 2,), 0, 1 << 20) % (margin + 1)
    lengths = lengths.at[donor].add(-passed).at[sink].add(passed)
    members = jnp.searchsorted(jnp.cumsum(lengths), jnp.arange(rows * top), side="right").astype(jnp.int32)
    table = members.reshape(top, rows).T
    table = table[jax.random.permutation(jax.random.fold_in(own, 1), rows)]
    rotation = jax.random.randint(jax.random.fold_in(own, 2), (rows, 1), 0, top)
    return jnp.take_along_axis(table, (jnp.arange(top)[None, :] + rotation) % top, axis=1)


def load_shares(amount, total, reach, lean, full):
    loads = [(1 << 20) // math.isqrt(rank ** lean) + 1 for rank in range(1, amount + 1)]
    largest = reach if full else min(reach, max(-(-total // amount), total * loads[0] // sum(loads)))
    least = 1 if total - largest >= amount - 1 else 0
    holding, surplus = [largest] + [least] * (amount - 1), total - largest - least * (amount - 1)
    while surplus > 0:
        movable = [i for i in range(1, amount) if holding[i] < largest] or [i for i in range(1, amount) if holding[i] < reach]
        pool, budget = sum([loads[i] for i in movable]), surplus
        for i in movable:
            more = min(reach - holding[i], max(1, budget * loads[i] // pool), surplus)
            holding[i] = holding[i] + more
            surplus = surplus - more
    return np.array(holding)


def scatter_about(rng, shape, width, reach, pieces=(), held_as=jnp.bfloat16):
    gain = shard_levels(rng, shape, pieces, -0.22, 0.18) if pieces else 1.0
    entries = jax.random.normal(rng, shape, jnp.float32) * width * gain
    return jnp.minimum(jnp.maximum(entries, -reach), reach).astype(held_as)


def setup_inputs(seed: int = 0) -> dict:
    keys = jax.random.split(jax.random.key(seed), 10)
    tokens = scatter_about(keys[0], (ROWS, MODEL_WIDTH), 1.0, 6.0, ((0, 256),))
    chosen_expert_index_keys = jax.random.split(jax.random.fold_in(keys[1], 1), ROWS // ROWS_DEV)
    chosen_expert_index_turns = jax.random.permutation(jax.random.fold_in(keys[1], 3), ROWS // ROWS_DEV)
    chosen_expert_index = jax.vmap(lambda own, number: deal_out(jax.random.fold_in(keys[1], 2), own, number, ROWS_DEV, EXPERTS, TOP, CAP, 2))(chosen_expert_index_keys, chosen_expert_index_turns).reshape((ROWS, TOP))
    expert_mixing_weight = jnp.clip(0.099609375 + 0.49804688 * jax.random.uniform(keys[2], (ROWS, TOP), jnp.float32) ** shard_levels(keys[2], (ROWS, TOP), ((0, 256),), -0.2, 0.2), 0.099609375, 0.59765625).astype(jnp.bfloat16)
    row_adapter_index = touch_ends(jax.random.randint(keys[3], (ROWS,), 0, ADAPTER_COUNT), jax.random.fold_in(keys[3], 1), 0, ADAPTER_COUNT - 1).astype(jnp.int32)
    gate_weight = scatter_about(keys[4], (EXPERTS, MODEL_WIDTH, HIDDEN_WIDTH), MODEL_WIDTH ** -0.5, 0.09375, ((0, 64), (2, 4)))
    up_weight = scatter_about(keys[5], (EXPERTS, MODEL_WIDTH, HIDDEN_WIDTH), MODEL_WIDTH ** -0.5, 0.09375, ((0, 64), (2, 4)))
    down_weight = scatter_about(keys[6], (EXPERTS, HIDDEN_WIDTH, MODEL_WIDTH), HIDDEN_WIDTH ** -0.5, 0.1875, ((0, 64), (2, 4)))
    adapter_down_factor = scatter_about(keys[7], (MODEL_WIDTH, ADAPTER_COUNT * ADAPTER_RANK), MODEL_WIDTH ** -0.5, 0.09375)
    adapter_up_factor = scatter_about(keys[8], (ADAPTER_COUNT * ADAPTER_RANK, HIDDEN_WIDTH), (4 * ADAPTER_RANK) ** -0.5, 0.75, ((1, 4),))
    return {"tokens": tokens, "chosen_expert_index": chosen_expert_index, "expert_mixing_weight": expert_mixing_weight, "row_adapter_index": row_adapter_index, "gate_weight": gate_weight, "up_weight": up_weight, "down_weight": down_weight, "adapter_down_factor": adapter_down_factor, "adapter_up_factor": adapter_up_factor}


def reference(tokens, chosen_expert_index, expert_mixing_weight, row_adapter_index, gate_weight, up_weight, down_weight, adapter_down_factor, adapter_up_factor):
    row_total = tokens.shape[0]
    adapter_row_count = ADAPTER_COUNT * ADAPTER_RANK
    lane_adapter = jnp.arange(adapter_row_count, dtype=jnp.int32) // ADAPTER_RANK
    adapter_row_mask = (row_adapter_index[:, None] == lane_adapter[None, :]).astype(jnp.float32)
    lowrank_product = (jnp.dot(tokens, adapter_down_factor, preferred_element_type=jnp.float32) * adapter_row_mask).astype(jnp.bfloat16)
    bound_rows = CAP * N_REP * N_EP

    def per_expert(accumulated, expert_index):
        matches = chosen_expert_index == expert_index
        chosen = jnp.any(matches, axis=1)
        weight = jnp.sum(jnp.where(matches, expert_mixing_weight.astype(jnp.float32), jnp.float32(0.0)), axis=1)
        (row_index,) = jnp.nonzero(chosen, size=bound_rows, fill_value=0)
        row_index = row_index.astype(jnp.int32)
        is_valid = jnp.arange(bound_rows, dtype=jnp.int32) < jnp.sum(chosen.astype(jnp.int32))
        picked_rows = tokens[row_index]
        picked_lowrank = lowrank_product[row_index]
        gate_value = jnp.dot(picked_rows, gate_weight[expert_index], preferred_element_type=jnp.float32)
        up_projection_value = jnp.dot(picked_rows, up_weight[expert_index], preferred_element_type=jnp.float32) + jnp.dot(picked_lowrank, adapter_up_factor, preferred_element_type=jnp.float32)
        hidden = (jax.nn.silu(gate_value) * up_projection_value).astype(jnp.bfloat16)
        expert_out = jnp.dot(hidden, down_weight[expert_index], preferred_element_type=jnp.float32).astype(jnp.bfloat16)
        row_scale = jnp.where(is_valid, weight[row_index], jnp.float32(0.0))
        accumulated = accumulated.at[row_index].add(row_scale[:, None] * expert_out.astype(jnp.float32))
        return accumulated, None

    mixed_sum, unused_out = lax.scan(per_expert, jnp.zeros((row_total, MODEL_WIDTH), jnp.float32), jnp.arange(EXPERTS, dtype=jnp.int32))
    return mixed_sum.astype(jnp.bfloat16)
```

```python
import jax
import jax.numpy as jnp
from jax import lax
from jax.sharding import PartitionSpec as P

ADAPTER_RANK = 16


def per_device(
    tokens,
    chosen_expert_index,
    expert_mixing_weight,
    row_adapter_index,
    gate_weight,
    up_weight,
    down_weight,
    adapter_down_factor,
    adapter_up_factor,
):
    row_count, width = tokens.shape
    owners = lax.axis_size("ep")
    groups = lax.axis_size("rep")
    local_count = gate_weight.shape[0]
    experts = local_count * owners
    capacity = 2
    share = down_weight.shape[2]
    f32 = jnp.float32
    bf16 = jnp.bfloat16

    flat_ids = chosen_expert_index.reshape(-1)
    one_hot = (flat_ids[:, None] == lax.iota(jnp.int32, experts)[None, :]).astype(jnp.int32)
    before = jnp.cumsum(one_hot, axis=0) - one_hot
    position = jnp.sum(before * one_hot, axis=1).reshape(chosen_expert_index.shape)
    local = chosen_expert_index % local_count
    owner = chosen_expert_index // local_count

    adapters = adapter_down_factor.shape[1]
    lane_adapter = lax.iota(jnp.int32, adapters) // ADAPTER_RANK
    adapter_mask = (row_adapter_index[:, None] == lane_adapter[None, :]).astype(f32)
    low = (
        jnp.dot(tokens, adapter_down_factor, preferred_element_type=f32) * adapter_mask
    ).astype(bf16)
    rows = jnp.concatenate([tokens, low], axis=1)

    slots = owners * capacity
    slot = owner * capacity + position
    mixing = expert_mixing_weight.astype(f32)
    received, combiners = [], []
    for j in range(local_count):
        matches = (slot[:, :, None] == lax.iota(jnp.int32, slots)[None, None, :]) & (
            local == j
        )[:, :, None]
        routing = jnp.any(matches, axis=1).astype(bf16)
        combiners.append(
            jnp.sum(jnp.where(matches, mixing[:, :, None], f32(0.0)), axis=1).astype(bf16)
        )
        packed = jnp.einsum("ri,rd->id", routing, rows, preferred_element_type=f32).astype(bf16)
        packed = packed.reshape(owners, capacity, width + adapters)
        received.append(lax.all_to_all(packed, "ep", split_axis=0, concat_axis=0, tiled=True))
    combiner = lax.all_gather(jnp.stack(combiners), "rep", axis=0)

    total = jnp.zeros((groups, row_count, share), f32)
    for j in range(local_count):
        mine = received[j].reshape(slots, width + adapters)
        every = lax.all_gather(mine, "rep", axis=0, tiled=True)
        row_part, low_part = every[:, :width], every[:, width:]
        gate = jnp.dot(row_part, gate_weight[j], preferred_element_type=f32)
        up = jnp.dot(row_part, up_weight[j], preferred_element_type=f32) + jnp.dot(
            low_part, adapter_up_factor, preferred_element_type=f32
        )
        hidden = (jax.nn.silu(gate) * up).astype(bf16)
        hidden = lax.all_gather(hidden, "rep", axis=1, tiled=True)
        out = jnp.dot(hidden, down_weight[j], preferred_element_type=f32).astype(bf16)
        out = out.reshape(groups, owners, capacity, share).transpose(1, 0, 2, 3)
        back = lax.all_to_all(out, "ep", split_axis=0, concat_axis=0, tiled=True)
        back = back.transpose(1, 0, 2, 3).reshape(groups, slots, share)
        total = total + jnp.einsum(
            "gri,gid->grd", combiner[:, j], back, preferred_element_type=f32
        )
    mixed = total.astype(bf16)
    mixed = lax.all_to_all(mixed, "rep", split_axis=0, concat_axis=0, tiled=True)
    return mixed.transpose(1, 0, 2).reshape(row_count, width)


def solution(mesh):
    placed = (
        P(("rep", "ep"), None),
        P(("rep", "ep"), None),
        P(("rep", "ep"), None),
        P(("rep", "ep")),
        P("ep", None, "rep"),
        P("ep", None, "rep"),
        P("ep", None, "rep"),
        P(),
        P(None, "rep"),
    )
    return jax.shard_map(
        per_device, mesh=mesh, in_specs=placed, out_specs=P(("rep", "ep"), None), check_vma=False
    )
```

```python
import functools

import jax
import jax.numpy as jnp
from jax import lax
from jax.experimental import pallas as pl
from jax.experimental.pallas import tpu as pltpu
from jax.sharding import PartitionSpec as P

ADAPTER_RANK = 16
VMEM_LIMIT = 40 * 1024 * 1024


def gate_up_kernel(parts, *refs):
    rows = refs[:parts]
    lows = refs[parts : 2 * parts]
    gate_ref, up_ref, factor_ref, _, hidden_ref, gate_sum, up_sum = refs[2 * parts :]
    step = pl.program_id(0)
    x = jnp.concatenate([r[...] for r in rows], axis=0) if parts > 1 else rows[0][...]
    gate = jnp.dot(x, gate_ref[0], preferred_element_type=jnp.float32)
    up = jnp.dot(x, up_ref[0], preferred_element_type=jnp.float32)

    @pl.when(step == 0)
    def _():
        low = jnp.concatenate([r[...] for r in lows], axis=0) if parts > 1 else lows[0][...]
        gate_sum[...] = gate
        up_sum[...] = up + jnp.dot(low, factor_ref[...], preferred_element_type=jnp.float32)

    @pl.when(step > 0)
    def _():
        gate_sum[...] += gate
        up_sum[...] += up

    @pl.when(step == pl.num_programs(0) - 1)
    def _():
        g = gate_sum[...]
        hidden_ref[...] = (g / (1.0 + jnp.exp(-g)) * up_sum[...]).astype(hidden_ref.dtype)


def gate_up(rows, gate_weight, up_weight, factor, expert, after):
    width, units = gate_weight.shape[1:]
    adapters = factor.shape[0]
    steps = 4
    depth = width // steps
    count = sum(r.shape[0] for r in rows)
    weight = pl.BlockSpec((1, depth, units), lambda k: (expert, k, 0))
    return pl.pallas_call(
        functools.partial(gate_up_kernel, len(rows)),
        grid=(steps,),
        in_specs=[pl.BlockSpec((r.shape[0], depth), lambda k: (0, k)) for r in rows]
        + [pl.BlockSpec((r.shape[0], adapters), lambda k: (0, width // adapters)) for r in rows]
        + [weight, weight, pl.BlockSpec((adapters, units), lambda k: (0, 0))]
        + [pl.BlockSpec(memory_space=pl.ANY)],
        out_specs=pl.BlockSpec((count, units), lambda k: (0, 0)),
        out_shape=jax.ShapeDtypeStruct((count, units), jnp.bfloat16),
        scratch_shapes=[pltpu.VMEM((count, units), jnp.float32)] * 2,
        compiler_params=pltpu.CompilerParams(vmem_limit_bytes=VMEM_LIMIT),
        cost_estimate=pl.CostEstimate(
            flops=4 * count * width * units,
            bytes_accessed=2 * (count * width + 2 * width * units + count * units),
            transcendentals=count * units,
        ),
        name="gate_up",
    )(*rows, *rows, gate_weight, up_weight, factor, after)


def down_kernel(groups, _, *refs):
    hidden, weights, out_ref = refs[:groups], refs[groups : 2 * groups], refs[2 * groups]
    out_ref[...] = sum(
        jnp.dot(h[...], w[0], preferred_element_type=jnp.float32)
        for h, w in zip(hidden, weights)
    ).astype(out_ref.dtype)


def down(hidden, down_weight, me, expert, turned):
    groups = len(hidden)
    count, units = hidden[0].shape
    share = down_weight.shape[2]
    block = count // groups
    if turned:
        from_at = [lambda i, m, s=s: ((i + groups - s) % groups, 0) for s in range(groups)]
        to_at = lambda i, m: ((m[0] + i) % groups, 0)
    else:
        from_at = [lambda i, m: (i, 0)] * groups
        to_at = lambda i, m: (i, 0)
    return pl.pallas_call(
        functools.partial(down_kernel, groups),
        grid_spec=pltpu.PrefetchScalarGridSpec(
            num_scalar_prefetch=1,
            grid=(groups,),
            in_specs=[pl.BlockSpec((block, units), at) for at in from_at]
            + [
                pl.BlockSpec(
                    (1, units, share), lambda i, m, s=s: (expert, (m[0] + s) % groups, 0)
                )
                for s in range(groups)
            ],
            out_specs=pl.BlockSpec((block, share), to_at),
        ),
        out_shape=jax.ShapeDtypeStruct((count, share), jnp.bfloat16),
        compiler_params=pltpu.CompilerParams(vmem_limit_bytes=VMEM_LIMIT),
        cost_estimate=pl.CostEstimate(
            flops=2 * count * units * groups * share,
            bytes_accessed=2 * (groups * count * units + groups * units * share + count * share),
            transcendentals=0,
        ),
        name="down",
    )(me, *hidden, *([down_weight] * groups))


def from_further(x, by):
    n = lax.axis_size("rep")
    return lax.ppermute(x, "rep", [(i, (i - by) % n) for i in range(n)])


def per_device(
    tokens,
    chosen_expert_index,
    expert_mixing_weight,
    row_adapter_index,
    gate_weight,
    up_weight,
    down_weight,
    adapter_down_factor,
    adapter_up_factor,
):
    row_count, width = tokens.shape
    owners = lax.axis_size("ep")
    groups = lax.axis_size("rep")
    local_count = gate_weight.shape[0]
    experts = local_count * owners
    capacity = 2
    share = down_weight.shape[2]
    f32 = jnp.float32
    bf16 = jnp.bfloat16

    flat_ids = chosen_expert_index.reshape(-1)
    one_hot = (flat_ids[:, None] == lax.iota(jnp.int32, experts)[None, :]).astype(jnp.int32)
    before = jnp.cumsum(one_hot, axis=0) - one_hot
    position = jnp.sum(before * one_hot, axis=1).reshape(chosen_expert_index.shape)
    local = chosen_expert_index % local_count
    owner = chosen_expert_index // local_count

    adapters = adapter_down_factor.shape[1]
    lane_adapter = lax.iota(jnp.int32, adapters) // ADAPTER_RANK
    adapter_mask = (row_adapter_index[:, None] == lane_adapter[None, :]).astype(f32)
    low = (
        jnp.dot(tokens, adapter_down_factor, preferred_element_type=f32) * adapter_mask
    ).astype(bf16)
    rows = jnp.concatenate([tokens, low], axis=1)

    slots = owners * capacity
    slot = owner * capacity + position
    mixing = expert_mixing_weight.astype(f32)
    received, combiners = [], []
    for j in range(local_count):
        matches = (slot[:, :, None] == lax.iota(jnp.int32, slots)[None, None, :]) & (
            local == j
        )[:, :, None]
        routing = jnp.any(matches, axis=1).astype(bf16)
        combiners.append(
            jnp.sum(jnp.where(matches, mixing[:, :, None], f32(0.0)), axis=1).astype(bf16)
        )
        packed = jnp.einsum("ri,rd->id", routing, rows, preferred_element_type=f32).astype(bf16)
        packed = packed.reshape(owners, capacity, width + adapters)
        sent = lax.all_to_all(packed, "ep", split_axis=0, concat_axis=0, tiled=True)
        received.append(sent.reshape(slots, width + adapters))

    me = lax.axis_index("rep").astype(jnp.int32).reshape(1)
    total = jnp.zeros((row_count, groups, share), f32)
    after = adapter_up_factor
    for j in range(local_count):
        mine = received[j]
        last = j == local_count - 1
        if last:
            half = slots // 2
            before_me, after_me = from_further(mine, -1), from_further(mine, 1)
            across = [from_further(before_me[:half], -1), from_further(after_me[half:], 1)]
            every = [mine, after_me, *across, before_me]
        else:
            every = [lax.all_gather(mine, "rep", axis=0, tiled=True)]
        hidden = gate_up(every, gate_weight, up_weight, adapter_up_factor, j, after)
        hidden = [hidden] + [from_further(hidden, s) for s in range(1, groups)]
        out = down(hidden, down_weight, me, j, last)
        after = out[:16, :128]
        out = out.reshape(groups * owners, capacity, share)
        back = lax.all_to_all(out, ("rep", "ep"), split_axis=0, concat_axis=0, tiled=True)
        back = back.reshape(groups, slots, share)
        total = total + jnp.einsum(
            "ri,gid->rgd", combiners[j], back, preferred_element_type=f32
        )
    return total.astype(bf16).reshape(row_count, width)


def solution(mesh):
    placed = (
        P(("rep", "ep"), None),
        P(("rep", "ep"), None),
        P(("rep", "ep"), None),
        P(("rep", "ep")),
        P("ep", None, "rep"),
        P("ep", None, "rep"),
        P("ep", None, "rep"),
        P(),
        P(None, "rep"),
    )
    return jax.shard_map(
        per_device, mesh=mesh, in_specs=placed, out_specs=P(("rep", "ep"), None), check_vma=False
    )
```

```python
import functools

import jax
import jax.numpy as jnp
from jax import lax
from jax.experimental import pallas as pl
from jax.experimental.pallas import tpu as pltpu
from jax.sharding import PartitionSpec as P

ADAPTER_RANK = 16
VMEM_LIMIT = 57 * 1024 * 1024


def gate_up_kernel(parts, expert, chunks, *refs):
    rows = refs[:parts]
    gate_ref, up_ref, factor_ref = refs[parts : parts + 3]
    hidden_ref, x, gate_at, up_at, factor_at, sems = refs[-6:]
    width, adapters = gate_ref.shape[1], factor_ref.shape[0]
    depth = width // chunks
    copies = []
    for c in range(chunks):
        here = pl.ds(c * depth, depth)
        wide = here if c < chunks - 1 else pl.ds(c * depth, depth + adapters)
        pairs, row = [], 0
        for part in rows:
            count = part.shape[0]
            pairs.append((part.at[:, wide], x.at[pl.ds(row, count), wide]))
            row += count
        pairs.append((gate_ref.at[expert, here], gate_at.at[here]))
        pairs.append((up_ref.at[expert, here], up_at.at[here]))
        if c == 0:
            pairs.append((factor_ref, factor_at))
        started = [
            pltpu.make_async_copy(src, dst, sems.at[c, i]) for i, (src, dst) in enumerate(pairs)
        ]
        for copy in started:
            copy.start()
        copies.append(started)
    gate = up = 0.0
    for c in range(chunks):
        for copy in copies[c]:
            copy.wait()
        here = slice(c * depth, (c + 1) * depth)
        gate += jnp.dot(x[:, here], gate_at[here], preferred_element_type=jnp.float32)
        up += jnp.dot(x[:, here], up_at[here], preferred_element_type=jnp.float32)
    up += jnp.dot(x[:, width:], factor_at[...], preferred_element_type=jnp.float32)
    hidden_ref[...] = (gate / (1.0 + jnp.exp(-gate)) * up).astype(hidden_ref.dtype)


def gate_up(rows, gate_weight, up_weight, factor, expert, after):
    width, units = gate_weight.shape[1:]
    adapters = factor.shape[0]
    chunks = 7
    parts = len(rows)
    count = sum(r.shape[0] for r in rows)
    anywhere = pl.BlockSpec(memory_space=pl.ANY)
    return pl.pallas_call(
        functools.partial(gate_up_kernel, parts, expert, chunks),
        in_specs=[anywhere] * (parts + 3 + len(after)),
        out_shape=jax.ShapeDtypeStruct((count, units), jnp.bfloat16),
        scratch_shapes=[
            pltpu.VMEM((count, width + adapters), jnp.bfloat16),
            pltpu.VMEM((width, units), jnp.bfloat16),
            pltpu.VMEM((width, units), jnp.bfloat16),
            pltpu.VMEM((adapters, units), jnp.bfloat16),
            pltpu.SemaphoreType.DMA((chunks, parts + 3)),
        ],
        compiler_params=pltpu.CompilerParams(vmem_limit_bytes=VMEM_LIMIT),
        cost_estimate=pl.CostEstimate(flops=1000, bytes_accessed=1000, transcendentals=0),
        name="gate_up",
    )(*rows, gate_weight, up_weight, factor, *after)


def down_kernel(groups, experts, me_ref, *refs):
    hidden = [refs[e * groups : (e + 1) * groups] for e in range(experts)]
    weight_ref = refs[experts * groups]
    out_ref, x, weight_at, sems = refs[-4:]
    count, units = hidden[0][0].shape
    block = count // groups
    me = me_ref[0]
    copies = []
    for e in range(experts):
        started = []
        for s in range(groups):
            owner = lax.rem(me + s, groups)
            started.append(
                pltpu.make_async_copy(
                    weight_ref.at[e, pl.ds(pl.multiple_of(owner * units, units), units)],
                    weight_at.at[e, pl.ds(s * units, units)],
                    sems.at[e, s, groups],
                )
            )
            for i in range(groups):
                started.append(
                    pltpu.make_async_copy(
                        hidden[e][s].at[pl.ds((i - s) % groups * block, block)],
                        x.at[e, pl.ds(i * block, block), pl.ds(s * units, units)],
                        sems.at[e, s, i],
                    )
                )
        for copy in started:
            copy.start()
        copies.append(started)
    for e in range(experts):
        for copy in copies[e]:
            copy.wait()
        out = jnp.dot(x[e], weight_at[e], preferred_element_type=jnp.float32)
        out = out.astype(out_ref.dtype)
        senders = block // out_ref.shape[2]
        for i in range(groups):
            at = pl.ds(lax.rem(me + i, groups) * senders, senders)
            rows = out[i * block : (i + 1) * block]
            out_ref[at, e] = rows.reshape((senders,) + out_ref.shape[2:])


def down(hidden, down_weight, me, capacity):
    experts, groups = len(hidden), len(hidden[0])
    count, units = hidden[0][0].shape
    share = down_weight.shape[2]
    anywhere = pl.BlockSpec(memory_space=pl.ANY)
    return pl.pallas_call(
        functools.partial(down_kernel, groups, experts),
        in_specs=[pl.BlockSpec(memory_space=pltpu.SMEM)]
        + [anywhere] * (groups * experts + 1),
        out_shape=jax.ShapeDtypeStruct((count // capacity, experts, capacity, share), jnp.bfloat16),
        scratch_shapes=[
            pltpu.VMEM((experts, count, groups * units), jnp.bfloat16),
            pltpu.VMEM((experts, groups * units, share), jnp.bfloat16),
            pltpu.SemaphoreType.DMA((experts, groups, groups + 1)),
        ],
        compiler_params=pltpu.CompilerParams(vmem_limit_bytes=VMEM_LIMIT),
        cost_estimate=pl.CostEstimate(flops=1000, bytes_accessed=1000, transcendentals=0),
        name="down",
    )(me, *[h for of_expert in hidden for h in of_expert], down_weight)


def relayout_kernel(x_ref, *refs):
    refs[-1][...] = x_ref[...].reshape(refs[-1].shape)


def relayout(x, shape, after):
    return pl.pallas_call(
        relayout_kernel,
        in_specs=[pl.BlockSpec(memory_space=pltpu.VMEM)]
        + [pl.BlockSpec(memory_space=pl.ANY)] * len(after),
        out_shape=jax.ShapeDtypeStruct(shape, x.dtype),
        compiler_params=pltpu.CompilerParams(vmem_limit_bytes=VMEM_LIMIT),
        cost_estimate=pl.CostEstimate(flops=1000, bytes_accessed=1000, transcendentals=0),
        name="relayout",
    )(x, *after)


def halves_kernel(half, before_ref, after_ref, *refs):
    top_ref, bottom_ref = refs[-2:]
    top_ref[...] = before_ref[:half]
    bottom_ref[...] = after_ref[half:]


def halves(before_me, after_me, after):
    count, width = before_me.shape
    half = count // 2
    vmem = pl.BlockSpec(memory_space=pltpu.VMEM)
    return pl.pallas_call(
        functools.partial(halves_kernel, half),
        in_specs=[vmem, vmem] + [pl.BlockSpec(memory_space=pl.ANY)] * len(after),
        out_shape=[jax.ShapeDtypeStruct((half, width), before_me.dtype)] * 2,
        compiler_params=pltpu.CompilerParams(vmem_limit_bytes=VMEM_LIMIT),
        cost_estimate=pl.CostEstimate(flops=1000, bytes_accessed=1000, transcendentals=0),
        name="halves",
    )(before_me, after_me, *after)


def from_further(x, by):
    n = lax.axis_size("rep")
    return lax.ppermute(x, "rep", [(i, (i - by) % n) for i in range(n)])


def per_device(
    tokens,
    chosen_expert_index,
    expert_mixing_weight,
    row_adapter_index,
    gate_weight,
    up_weight,
    down_weight,
    adapter_down_factor,
    adapter_up_factor,
):
    row_count, width = tokens.shape
    owners = lax.axis_size("ep")
    groups = lax.axis_size("rep")
    local_count = gate_weight.shape[0]
    experts = local_count * owners
    capacity = 2
    share = down_weight.shape[2]
    f32 = jnp.float32
    bf16 = jnp.bfloat16

    flat_ids = chosen_expert_index.reshape(-1)
    one_hot = (flat_ids[:, None] == lax.iota(jnp.int32, experts)[None, :]).astype(jnp.int32)
    before = jnp.cumsum(one_hot, axis=0) - one_hot
    position = jnp.sum(before * one_hot, axis=1).reshape(chosen_expert_index.shape)
    local = chosen_expert_index % local_count
    owner = chosen_expert_index // local_count

    adapters = adapter_down_factor.shape[1]
    lane_adapter = lax.iota(jnp.int32, adapters) // ADAPTER_RANK
    adapter_mask = (row_adapter_index[:, None] == lane_adapter[None, :]).astype(f32)
    low = (
        jnp.dot(tokens, adapter_down_factor, preferred_element_type=f32) * adapter_mask
    ).astype(bf16)
    rows = jnp.concatenate([tokens, low], axis=1)

    slots = owners * capacity
    slot = owner * capacity + position
    mixing = expert_mixing_weight.astype(f32)
    received, combiners = [], []
    for j in range(local_count):
        matches = (slot[:, :, None] == lax.iota(jnp.int32, slots)[None, None, :]) & (
            local == j
        )[:, :, None]
        routing = jnp.any(matches, axis=1).astype(bf16)
        combiners.append(
            jnp.sum(jnp.where(matches, mixing[:, :, None], f32(0.0)), axis=1).astype(bf16)
        )
        packed = jnp.einsum("ri,rd->id", routing, rows, preferred_element_type=f32).astype(bf16)
        packed = packed.reshape(owners, capacity, width + adapters)
        sent = lax.all_to_all(packed, "ep", split_axis=0, concat_axis=0, tiled=True)
        received.append(sent)

    me = lax.axis_index("rep").astype(jnp.int32).reshape(1)
    half = slots // 2
    hidden = []
    for j, sent in enumerate(received):
        mine = relayout(sent, (slots, width + adapters), [])
        before_me, after_me = from_further(mine, -1), from_further(mine, 1)
        across = [from_further(before_me[:half], -1), from_further(after_me[half:], 1)]
        every = [mine, after_me, *across, before_me]
        units = gate_up(every, gate_weight, up_weight, adapter_up_factor, j, [])
        hidden.append([units] + [from_further(units, s) for s in range(1, groups)])
    back = down(hidden, down_weight, me, capacity)
    back = lax.all_to_all(back, ("rep", "ep"), split_axis=0, concat_axis=0, tiled=True)
    back = back.reshape(groups, owners * local_count * capacity, share)
    combiner = jnp.stack([c.reshape(row_count, owners, capacity) for c in combiners], axis=2)
    total = jnp.einsum(
        "ri,gid->rgd", combiner.reshape(row_count, -1), back, preferred_element_type=f32
    )
    return total.astype(bf16).reshape(row_count, width)


def solution(mesh):
    placed = (
        P(("rep", "ep"), None),
        P(("rep", "ep"), None),
        P(("rep", "ep"), None),
        P(("rep", "ep")),
        P("ep", None, "rep"),
        P("ep", None, "rep"),
        P("ep", None, "rep"),
        P(),
        P(None, "rep"),
    )
    return jax.shard_map(
        per_device, mesh=mesh, in_specs=placed, out_specs=P(("rep", "ep"), None), check_vma=False
    )
```

```python
import functools

import jax
import jax.numpy as jnp
from jax import lax
from jax.experimental import pallas as pl
from jax.experimental.pallas import tpu as pltpu
from jax.sharding import PartitionSpec as P

ADAPTER_RANK = 16
VMEM_LIMIT = 16 * 1024 * 1024


def gate_up_kernel(parts, expert, chunks, *refs):
    rows = refs[:parts]
    gate_ref, up_ref, factor_ref = refs[parts : parts + 3]
    hidden_ref, x, gate_at, up_at, factor_at, sems = refs[-6:]
    width, adapters = gate_ref.shape[1], factor_ref.shape[0]
    depth = width // chunks
    copies = []
    for c in range(chunks):
        here = pl.ds(c * depth, depth)
        wide = here if c < chunks - 1 else pl.ds(c * depth, depth + adapters)
        pairs, row = [], 0
        for part in rows:
            count = part.shape[0]
            pairs.append((part.at[:, wide], x.at[pl.ds(row, count), wide]))
            row += count
        pairs.append((gate_ref.at[expert, here], gate_at.at[here]))
        pairs.append((up_ref.at[expert, here], up_at.at[here]))
        if c == 0:
            pairs.append((factor_ref, factor_at))
        started = [
            pltpu.make_async_copy(src, dst, sems.at[c, i]) for i, (src, dst) in enumerate(pairs)
        ]
        for copy in started:
            copy.start()
        copies.append(started)
    gate = up = 0.0
    for c in range(chunks):
        for copy in copies[c]:
            copy.wait()
        here = slice(c * depth, (c + 1) * depth)
        gate += jnp.dot(x[:, here], gate_at[here], preferred_element_type=jnp.float32)
        up += jnp.dot(x[:, here], up_at[here], preferred_element_type=jnp.float32)
    up += jnp.dot(x[:, width:], factor_at[...], preferred_element_type=jnp.float32)
    hidden_ref[...] = (gate / (1.0 + jnp.exp(-gate)) * up).astype(hidden_ref.dtype)


def gate_up(rows, gate_weight, up_weight, factor, expert, after):
    width, units = gate_weight.shape[1:]
    adapters = factor.shape[0]
    chunks = 7
    parts = len(rows)
    count = sum(r.shape[0] for r in rows)
    anywhere = pl.BlockSpec(memory_space=pl.ANY)
    return pl.pallas_call(
        functools.partial(gate_up_kernel, parts, expert, chunks),
        in_specs=[anywhere] * (parts + 3 + len(after)),
        out_shape=jax.ShapeDtypeStruct((count, units), jnp.bfloat16),
        scratch_shapes=[
            pltpu.VMEM((count, width + adapters), jnp.bfloat16),
            pltpu.VMEM((width, units), jnp.bfloat16),
            pltpu.VMEM((width, units), jnp.bfloat16),
            pltpu.VMEM((adapters, units), jnp.bfloat16),
            pltpu.SemaphoreType.DMA((chunks, parts + 3)),
        ],
        compiler_params=pltpu.CompilerParams(vmem_limit_bytes=VMEM_LIMIT),
        cost_estimate=pl.CostEstimate(flops=1000, bytes_accessed=1000, transcendentals=0),
        name="gate_up",
    )(*rows, gate_weight, up_weight, factor, *after)


def down_kernel(groups, expert, me_ref, *refs):
    hidden, weight_ref = refs[:groups], refs[groups]
    out_ref, x, weight_at, made, sems = refs[-5:]
    count, units = hidden[0].shape
    block = count // groups
    me = me_ref[0]
    copies = []
    for s in range(groups):
        owner = lax.rem(me + s, groups)
        copies.append(
            pltpu.make_async_copy(
                weight_ref.at[expert, pl.ds(pl.multiple_of(owner * units, units), units)],
                weight_at.at[pl.ds(s * units, units)],
                sems.at[s, groups],
            )
        )
        for i in range(groups):
            copies.append(
                pltpu.make_async_copy(
                    hidden[s].at[pl.ds((i - s) % groups * block, block)],
                    x.at[pl.ds(i * block, block), pl.ds(s * units, units)],
                    sems.at[s, i],
                )
            )
    for copy in copies:
        copy.start()
    for copy in copies:
        copy.wait()
    out = jnp.dot(x[...], weight_at[...], preferred_element_type=jnp.float32)
    out = out.astype(made.dtype)
    stored = []
    for i in range(groups):
        senders = block // made.shape[1]
        made[i * senders : (i + 1) * senders] = out[i * block : (i + 1) * block].reshape(
            (senders,) + made.shape[1:]
        )
        to = pl.ds(lax.rem(me + i, groups) * senders, senders)
        copy = pltpu.make_async_copy(
            made.at[pl.ds(i * senders, senders)], out_ref.at[to, expert], sems.at[groups, i]
        )
        copy.start()
        stored.append(copy)
    for copy in stored:
        copy.wait()


def down(hidden, down_weight, me, expert, capacity, outputs):
    groups = len(hidden)
    count, units = hidden[0].shape
    experts, share = down_weight.shape[0], down_weight.shape[2]
    anywhere = pl.BlockSpec(memory_space=pl.ANY)
    held = [] if outputs is None else [outputs]
    return pl.pallas_call(
        functools.partial(down_kernel, groups, expert),
        in_specs=[pl.BlockSpec(memory_space=pltpu.SMEM)]
        + [anywhere] * (groups + 1 + len(held)),
        out_specs=anywhere,
        out_shape=jax.ShapeDtypeStruct((count // capacity, experts, capacity, share), jnp.bfloat16),
        scratch_shapes=[
            pltpu.VMEM((count, groups * units), jnp.bfloat16),
            pltpu.VMEM((groups * units, share), jnp.bfloat16),
            pltpu.VMEM((count // capacity, capacity, share), jnp.bfloat16),
            pltpu.SemaphoreType.DMA((groups + 1, groups + 1)),
        ],
        input_output_aliases={groups + 2: 0} if held else {},
        compiler_params=pltpu.CompilerParams(vmem_limit_bytes=VMEM_LIMIT),
        cost_estimate=pl.CostEstimate(flops=1000, bytes_accessed=1000, transcendentals=0),
        name="down",
    )(me, *hidden, down_weight, *held)


def combine_kernel(groups, combiner_ref, back_ref, mixed_ref, held, sems):
    senders = held.shape[0] // groups
    share = held.shape[3]
    copies = []
    for g in range(groups):
        at = pl.ds(g * senders, senders)
        copy = pltpu.make_async_copy(back_ref.at[at], held.at[at], sems.at[g])
        copy.start()
        copies.append(copy)
    for g in range(groups):
        copies[g].wait()
        rows = held[g * senders : (g + 1) * senders]
        rows = rows.reshape((-1,) + rows.shape[2:]).reshape(-1, share)
        mixed_ref[:, g * share : (g + 1) * share] = jnp.dot(
            combiner_ref[...], rows, preferred_element_type=jnp.float32
        ).astype(mixed_ref.dtype)


def combine(combiner, back, groups):
    return pl.pallas_call(
        functools.partial(combine_kernel, groups),
        in_specs=[pl.BlockSpec(memory_space=pltpu.VMEM), pl.BlockSpec(memory_space=pl.ANY)],
        out_shape=jax.ShapeDtypeStruct((combiner.shape[0], groups * back.shape[3]), jnp.bfloat16),
        scratch_shapes=[
            pltpu.VMEM(back.shape, jnp.bfloat16),
            pltpu.SemaphoreType.DMA((groups,)),
        ],
        compiler_params=pltpu.CompilerParams(vmem_limit_bytes=VMEM_LIMIT),
        cost_estimate=pl.CostEstimate(flops=1000, bytes_accessed=1000, transcendentals=0),
        name="combine",
    )(combiner, back)


def relayout_kernel(x_ref, *refs):
    refs[-1][...] = x_ref[...].reshape(refs[-1].shape)


def relayout(x, shape, after):
    return pl.pallas_call(
        relayout_kernel,
        in_specs=[pl.BlockSpec(memory_space=pltpu.VMEM)]
        + [pl.BlockSpec(memory_space=pl.ANY)] * len(after),
        out_shape=jax.ShapeDtypeStruct(shape, x.dtype),
        compiler_params=pltpu.CompilerParams(vmem_limit_bytes=VMEM_LIMIT),
        cost_estimate=pl.CostEstimate(flops=1000, bytes_accessed=1000, transcendentals=0),
        name="relayout",
    )(x, *after)


def halves_kernel(half, before_ref, after_ref, *refs):
    top_ref, bottom_ref = refs[-2:]
    top_ref[...] = before_ref[:half]
    bottom_ref[...] = after_ref[half:]


def halves(before_me, after_me, after):
    count, width = before_me.shape
    half = count // 2
    vmem = pl.BlockSpec(memory_space=pltpu.VMEM)
    return pl.pallas_call(
        functools.partial(halves_kernel, half),
        in_specs=[vmem, vmem] + [pl.BlockSpec(memory_space=pl.ANY)] * len(after),
        out_shape=[jax.ShapeDtypeStruct((half, width), before_me.dtype)] * 2,
        compiler_params=pltpu.CompilerParams(vmem_limit_bytes=VMEM_LIMIT),
        cost_estimate=pl.CostEstimate(flops=1000, bytes_accessed=1000, transcendentals=0),
        name="halves",
    )(before_me, after_me, *after)


def from_further(x, by):
    n = lax.axis_size("rep")
    return lax.ppermute(x, "rep", [(i, (i - by) % n) for i in range(n)])


def per_device(
    tokens,
    chosen_expert_index,
    expert_mixing_weight,
    row_adapter_index,
    gate_weight,
    up_weight,
    down_weight,
    adapter_down_factor,
    adapter_up_factor,
):
    row_count, width = tokens.shape
    owners = lax.axis_size("ep")
    groups = lax.axis_size("rep")
    local_count = gate_weight.shape[0]
    experts = local_count * owners
    capacity = 2
    share = down_weight.shape[2]
    f32 = jnp.float32
    bf16 = jnp.bfloat16

    flat_ids = chosen_expert_index.reshape(-1)
    one_hot = (flat_ids[:, None] == lax.iota(jnp.int32, experts)[None, :]).astype(jnp.int32)
    before = jnp.cumsum(one_hot, axis=0) - one_hot
    position = jnp.sum(before * one_hot, axis=1).reshape(chosen_expert_index.shape)
    local = chosen_expert_index % local_count
    owner = chosen_expert_index // local_count

    adapters = adapter_down_factor.shape[1]
    lane_adapter = lax.iota(jnp.int32, adapters) // ADAPTER_RANK
    adapter_mask = (row_adapter_index[:, None] == lane_adapter[None, :]).astype(f32)
    low = (
        jnp.dot(tokens, adapter_down_factor, preferred_element_type=f32) * adapter_mask
    ).astype(bf16)
    rows = jnp.concatenate([tokens, low], axis=1)

    slots = owners * capacity
    slot = owner * capacity + position
    mixing = expert_mixing_weight.astype(f32)
    received, combiners = [], []
    for j in range(local_count):
        matches = (slot[:, :, None] == lax.iota(jnp.int32, slots)[None, None, :]) & (
            local == j
        )[:, :, None]
        routing = jnp.any(matches, axis=1).astype(bf16)
        combiners.append(
            jnp.sum(jnp.where(matches, mixing[:, :, None], f32(0.0)), axis=1).astype(bf16)
        )
        packed = jnp.einsum("ri,rd->id", routing, rows, preferred_element_type=f32).astype(bf16)
        packed = packed.reshape(owners, capacity, width + adapters)
        sent = lax.all_to_all(packed, "ep", split_axis=0, concat_axis=0, tiled=True)
        received.append(sent)

    gate_weight, up_weight, down_weight = (
        pltpu.with_memory_space_constraint(w, pltpu.HBM)
        for w in (gate_weight, up_weight, down_weight)
    )
    me = lax.axis_index("rep").astype(jnp.int32).reshape(1)
    half = slots // 2
    back = None
    for j, sent in enumerate(received):
        mine = relayout(sent, (slots, width + adapters), [])
        before_me, after_me = from_further(mine, -1), from_further(mine, 1)
        across = [from_further(before_me[:half], -1), from_further(after_me[half:], 1)]
        every = [mine, after_me, *across, before_me]
        units = gate_up(every, gate_weight, up_weight, adapter_up_factor, j, [])
        hidden = [units] + [from_further(units, s) for s in range(1, groups)]
        back = down(hidden, down_weight, me, j, capacity, back)
    back = lax.all_to_all(back, ("rep", "ep"), split_axis=0, concat_axis=0, tiled=True)
    combiner = jnp.stack([c.reshape(row_count, owners, capacity) for c in combiners], axis=2)
    return combine(combiner.reshape(row_count, -1), back, groups)


def solution(mesh):
    placed = (
        P(("rep", "ep"), None),
        P(("rep", "ep"), None),
        P(("rep", "ep"), None),
        P(("rep", "ep")),
        P("ep", None, "rep"),
        P("ep", None, "rep"),
        P("ep", None, "rep"),
        P(),
        P(None, "rep"),
    )
    return jax.shard_map(
        per_device, mesh=mesh, in_specs=placed, out_specs=P(("rep", "ep"), None), check_vma=False
    )
```

```python
import functools

import jax
import jax.numpy as jnp
from jax import lax
from jax.experimental import pallas as pl
from jax.experimental.pallas import tpu as pltpu
from jax.sharding import PartitionSpec as P

ADAPTER_RANK = 16
VMEM_LIMIT = 16 * 1024 * 1024


def in_vmem(x):
    return pltpu.with_memory_space_constraint(x, pltpu.VMEM)


def in_hbm(x):
    return pltpu.with_memory_space_constraint(x, pltpu.HBM)


def gate_up_kernel(parts, expert, chunks, *refs):
    rows = refs[:parts]
    gate_ref, up_ref, factor_ref, hidden_ref = refs[parts:]
    width = gate_ref.shape[1]
    depth = width // chunks
    low = jnp.concatenate([r[:, width:] for r in rows], axis=0)
    up = jnp.dot(low, factor_ref[...], preferred_element_type=jnp.float32)
    gate = 0.0
    for c in range(chunks):
        here = slice(c * depth, (c + 1) * depth)
        x = jnp.concatenate([r[:, here] for r in rows], axis=0)
        gate += jnp.dot(x, gate_ref[expert, here], preferred_element_type=jnp.float32)
        up += jnp.dot(x, up_ref[expert, here], preferred_element_type=jnp.float32)
    hidden_ref[...] = (gate / (1.0 + jnp.exp(-gate)) * up).astype(hidden_ref.dtype)


def gate_up(rows, gate_weight, up_weight, factor, expert, chunks=7):
    units = gate_weight.shape[2]
    parts = len(rows)
    count = sum(r.shape[0] for r in rows)
    vmem = pl.BlockSpec(memory_space=pltpu.VMEM)
    return pl.pallas_call(
        functools.partial(gate_up_kernel, parts, expert, chunks),
        in_specs=[vmem] * (parts + 3),
        out_specs=vmem,
        out_shape=jax.ShapeDtypeStruct((count, units), jnp.bfloat16),
        compiler_params=pltpu.CompilerParams(vmem_limit_bytes=VMEM_LIMIT),
        cost_estimate=pl.CostEstimate(flops=1000, bytes_accessed=1000, transcendentals=0),
        name="gate_up",
    )(*(in_vmem(x) for x in (*rows, gate_weight, up_weight)), factor)


def down_kernel(groups, expert, me_ref, *refs):
    hidden, weight_ref = refs[:groups], refs[groups]
    out_ref, made, sems = refs[-3:]
    count, units = hidden[0].shape
    block = count // groups
    me = me_ref[0]
    weights, columns = [], []
    for s in range(groups):
        at = pl.multiple_of(lax.rem(me + s, groups) * units, units)
        weights.append(weight_ref[expert, pl.ds(at, units)])
        turned = [(i - s) % groups * block for i in range(groups)]
        columns.append(jnp.concatenate([hidden[s][t : t + block] for t in turned], axis=0))
    out = jnp.dot(
        jnp.concatenate(columns, axis=1),
        jnp.concatenate(weights, axis=0),
        preferred_element_type=jnp.float32,
    )
    out = out.astype(made.dtype)
    stored = []
    for i in range(groups):
        senders = block // made.shape[1]
        made[i * senders : (i + 1) * senders] = out[i * block : (i + 1) * block].reshape(
            (senders,) + made.shape[1:]
        )
        to = pl.ds(lax.rem(me + i, groups) * senders, senders)
        copy = pltpu.make_async_copy(
            made.at[pl.ds(i * senders, senders)], out_ref.at[to, expert], sems.at[i]
        )
        copy.start()
        stored.append(copy)
    for copy in stored:
        copy.wait()


def down(hidden, down_weight, me, expert, capacity, outputs):
    groups = len(hidden)
    count, units = hidden[0].shape
    experts, share = down_weight.shape[0], down_weight.shape[2]
    anywhere = pl.BlockSpec(memory_space=pl.ANY)
    vmem = pl.BlockSpec(memory_space=pltpu.VMEM)
    held = [] if outputs is None else [outputs]
    return pl.pallas_call(
        functools.partial(down_kernel, groups, expert),
        in_specs=[pl.BlockSpec(memory_space=pltpu.SMEM)]
        + [vmem] * (groups + 1)
        + [anywhere] * len(held),
        out_specs=anywhere,
        out_shape=jax.ShapeDtypeStruct((count // capacity, experts, capacity, share), jnp.bfloat16),
        scratch_shapes=[
            pltpu.VMEM((count // capacity, capacity, share), jnp.bfloat16),
            pltpu.SemaphoreType.DMA((groups,)),
        ],
        input_output_aliases={groups + 2: 0} if held else {},
        compiler_params=pltpu.CompilerParams(vmem_limit_bytes=VMEM_LIMIT),
        cost_estimate=pl.CostEstimate(flops=1000, bytes_accessed=1000, transcendentals=0),
        name="down",
    )(me, *(in_vmem(x) for x in (*hidden, down_weight)), *held)


def combine_kernel(groups, combiner_ref, back_ref, mixed_ref):
    senders = back_ref.shape[0] // groups
    share = back_ref.shape[3]
    for g in range(groups):
        rows = back_ref[g * senders : (g + 1) * senders]
        rows = rows.reshape((-1,) + rows.shape[2:]).reshape(-1, share)
        mixed_ref[:, g * share : (g + 1) * share] = jnp.dot(
            combiner_ref[...], rows, preferred_element_type=jnp.float32
        ).astype(mixed_ref.dtype)


def combine(combiner, back, groups):
    vmem = pl.BlockSpec(memory_space=pltpu.VMEM)
    return pl.pallas_call(
        functools.partial(combine_kernel, groups),
        in_specs=[vmem, vmem],
        out_shape=jax.ShapeDtypeStruct((combiner.shape[0], groups * back.shape[3]), jnp.bfloat16),
        compiler_params=pltpu.CompilerParams(vmem_limit_bytes=VMEM_LIMIT),
        cost_estimate=pl.CostEstimate(flops=1000, bytes_accessed=1000, transcendentals=0),
        name="combine",
    )(combiner, in_vmem(back))


def relayout_kernel(x_ref, *refs):
    refs[-1][...] = x_ref[...].reshape(refs[-1].shape)


def relayout(x, shape, after):
    return pl.pallas_call(
        relayout_kernel,
        in_specs=[pl.BlockSpec(memory_space=pltpu.VMEM)]
        + [pl.BlockSpec(memory_space=pl.ANY)] * len(after),
        out_shape=jax.ShapeDtypeStruct(shape, x.dtype),
        compiler_params=pltpu.CompilerParams(vmem_limit_bytes=VMEM_LIMIT),
        cost_estimate=pl.CostEstimate(flops=1000, bytes_accessed=1000, transcendentals=0),
        name="relayout",
    )(x, *after)


def halves_kernel(half, before_ref, after_ref, *refs):
    top_ref, bottom_ref = refs[-2:]
    top_ref[...] = before_ref[:half]
    bottom_ref[...] = after_ref[half:]


def halves(before_me, after_me, after):
    count, width = before_me.shape
    half = count // 2
    vmem = pl.BlockSpec(memory_space=pltpu.VMEM)
    return pl.pallas_call(
        functools.partial(halves_kernel, half),
        in_specs=[vmem, vmem] + [pl.BlockSpec(memory_space=pl.ANY)] * len(after),
        out_shape=[jax.ShapeDtypeStruct((half, width), before_me.dtype)] * 2,
        compiler_params=pltpu.CompilerParams(vmem_limit_bytes=VMEM_LIMIT),
        cost_estimate=pl.CostEstimate(flops=1000, bytes_accessed=1000, transcendentals=0),
        name="halves",
    )(before_me, after_me, *after)


def pack_kernel(routing_ref, tokens_ref, down_ref, mask_ref, out_ref):
    tokens = tokens_ref[...]
    low = jnp.dot(tokens, down_ref[...], preferred_element_type=jnp.float32) * mask_ref[...]
    width = tokens.shape[1]
    share = width // 4
    for c in range(4):
        here = slice(c * share, (c + 1) * share)
        picked = jnp.dot(routing_ref[...], tokens[:, here], preferred_element_type=jnp.float32)
        out_ref[:, :, here] = picked.astype(out_ref.dtype).reshape(out_ref.shape[:2] + (share,))
    picked = jnp.dot(
        routing_ref[...], low.astype(out_ref.dtype), preferred_element_type=jnp.float32
    )
    out_ref[:, :, width:] = picked.astype(out_ref.dtype).reshape(
        out_ref.shape[:2] + (low.shape[1],)
    )


def pack(routing, tokens, adapter_down_factor, mask, owners):
    slots, adapters = routing.shape[0], mask.shape[1]
    vmem = pl.BlockSpec(memory_space=pltpu.VMEM)
    return pl.pallas_call(
        pack_kernel,
        in_specs=[vmem] * 4,
        out_shape=jax.ShapeDtypeStruct(
            (owners, slots // owners, tokens.shape[1] + adapters), jnp.bfloat16
        ),
        compiler_params=pltpu.CompilerParams(vmem_limit_bytes=VMEM_LIMIT),
        cost_estimate=pl.CostEstimate(flops=1000, bytes_accessed=1000, transcendentals=0),
        name="pack",
    )(routing, in_hbm(tokens), in_hbm(adapter_down_factor), mask)


def from_further(x, by):
    n = lax.axis_size("rep")
    return lax.ppermute(x, "rep", [(i, (i - by) % n) for i in range(n)])


def per_device(
    tokens,
    chosen_expert_index,
    expert_mixing_weight,
    row_adapter_index,
    gate_weight,
    up_weight,
    down_weight,
    adapter_down_factor,
    adapter_up_factor,
):
    row_count, width = tokens.shape
    owners = lax.axis_size("ep")
    groups = lax.axis_size("rep")
    local_count = gate_weight.shape[0]
    experts = local_count * owners
    capacity = 2
    share = down_weight.shape[2]
    f32 = jnp.float32
    bf16 = jnp.bfloat16

    flat_ids = chosen_expert_index.reshape(-1)
    one_hot = (flat_ids[:, None] == lax.iota(jnp.int32, experts)[None, :]).astype(jnp.int32)
    before = jnp.cumsum(one_hot, axis=0) - one_hot
    position = jnp.sum(before * one_hot, axis=1).reshape(chosen_expert_index.shape)
    local = chosen_expert_index % local_count
    owner = chosen_expert_index // local_count

    adapters = adapter_down_factor.shape[1]
    lane_adapter = lax.iota(jnp.int32, adapters) // ADAPTER_RANK
    adapter_mask = (row_adapter_index[:, None] == lane_adapter[None, :]).astype(f32)
    slots = owners * capacity
    slot = owner * capacity + position
    mixing = expert_mixing_weight.astype(f32)
    received, combiners = [], []
    for j in range(local_count):
        matches = (slot[:, :, None] == lax.iota(jnp.int32, slots)[None, None, :]) & (
            local == j
        )[:, :, None]
        routing = (
            (slot[None, :, :] == lax.iota(jnp.int32, slots)[:, None, None])
            & (local == j)[None, :, :]
        )
        routing = jnp.any(routing, axis=2).astype(bf16)
        combiners.append(
            jnp.sum(jnp.where(matches, mixing[:, :, None], f32(0.0)), axis=1).astype(bf16)
        )
        packed = pack(
            routing, tokens, adapter_down_factor, adapter_mask, owners
        )
        sent = lax.all_to_all(packed, "ep", split_axis=0, concat_axis=0, tiled=True)
        received.append(sent)

    me = lax.axis_index("rep").astype(jnp.int32).reshape(1)
    half = slots // 2
    back = None
    for j, sent in enumerate(received):
        mine = relayout(sent, (slots, width + adapters), [])
        before_me, after_me = from_further(mine, -1), from_further(mine, 1)
        across = [from_further(before_me[:half], -1), from_further(after_me[half:], 1)]
        every = [mine, after_me, *across, before_me]
        units = gate_up(every, gate_weight, up_weight, adapter_up_factor, j)
        hidden = [units] + [from_further(units, s) for s in range(1, groups)]
        back = down(hidden, down_weight, me, j, capacity, back)
    back = lax.all_to_all(back, ("rep", "ep"), split_axis=0, concat_axis=0, tiled=True)
    combiner = jnp.stack([c.reshape(row_count, owners, capacity) for c in combiners], axis=2)
    return combine(combiner.reshape(row_count, -1), back, groups)


def solution(mesh):
    placed = (
        P(("rep", "ep"), None),
        P(("rep", "ep"), None),
        P(("rep", "ep"), None),
        P(("rep", "ep")),
        P("ep", None, "rep"),
        P("ep", None, "rep"),
        P("ep", None, "rep"),
        P(),
        P(None, "rep"),
    )
    return jax.shard_map(
        per_device, mesh=mesh, in_specs=placed, out_specs=P(("rep", "ep"), None), check_vma=False
    )
```

```python
import functools

import jax
import jax.numpy as jnp
from jax import lax
from jax.experimental import pallas as pl
from jax.experimental.pallas import tpu as pltpu
from jax.sharding import PartitionSpec as P

ADAPTER_RANK = 16
VMEM_LIMIT = 16 * 1024 * 1024


def in_vmem(x):
    return pltpu.with_memory_space_constraint(x, pltpu.VMEM)


def in_hbm(x):
    return pltpu.with_memory_space_constraint(x, pltpu.HBM)


def gate_up_kernel(parts, expert, chunks, *refs):
    rows = refs[:parts]
    gate_ref, up_ref, factor_ref, hidden_ref = refs[parts:]
    width = gate_ref.shape[1]
    depth = width // chunks
    low = jnp.concatenate([r[:, width:] for r in rows], axis=0)
    up = jnp.dot(low, factor_ref[...], preferred_element_type=jnp.float32)
    gate = 0.0
    for c in range(chunks):
        here = slice(c * depth, (c + 1) * depth)
        x = jnp.concatenate([r[:, here] for r in rows], axis=0)
        gate += jnp.dot(x, gate_ref[expert, here], preferred_element_type=jnp.float32)
        up += jnp.dot(x, up_ref[expert, here], preferred_element_type=jnp.float32)
    hidden_ref[...] = (gate / (1.0 + jnp.exp(-gate)) * up).astype(hidden_ref.dtype)


def gate_up(rows, gate_weight, up_weight, factor, expert, chunks=7):
    units = gate_weight.shape[2]
    parts = len(rows)
    count = sum(r.shape[0] for r in rows)
    vmem = pl.BlockSpec(memory_space=pltpu.VMEM)
    return pl.pallas_call(
        functools.partial(gate_up_kernel, parts, expert, chunks),
        in_specs=[vmem] * (parts + 3),
        out_specs=vmem,
        out_shape=jax.ShapeDtypeStruct((count, units), jnp.bfloat16),
        compiler_params=pltpu.CompilerParams(vmem_limit_bytes=VMEM_LIMIT),
        cost_estimate=pl.CostEstimate(flops=1000, bytes_accessed=1000, transcendentals=0),
        name="gate_up",
    )(*(in_vmem(x) for x in (*rows, gate_weight, up_weight)), factor)


def down_kernel(groups, expert, me_ref, *refs):
    hidden, weight_ref = refs[:groups], refs[groups]
    out_ref, made, sems = refs[-3:]
    count, units = hidden[0].shape
    block = count // groups
    me = me_ref[0]
    weights, columns = [], []
    for s in range(groups):
        at = pl.multiple_of(lax.rem(me + s, groups) * units, units)
        weights.append(weight_ref[expert, pl.ds(at, units)])
        turned = [(i - s) % groups * block for i in range(groups)]
        columns.append(jnp.concatenate([hidden[s][t : t + block] for t in turned], axis=0))
    out = jnp.dot(
        jnp.concatenate(columns, axis=1),
        jnp.concatenate(weights, axis=0),
        preferred_element_type=jnp.float32,
    )
    out = out.astype(made.dtype)
    stored = []
    for i in range(groups):
        senders = block // made.shape[1]
        made[i * senders : (i + 1) * senders] = out[i * block : (i + 1) * block].reshape(
            (senders,) + made.shape[1:]
        )
        copy = pltpu.make_async_copy(
            made.at[pl.ds(i * senders, senders)],
            out_ref.at[:, lax.rem(me + i, groups), expert],
            sems.at[i],
        )
        copy.start()
        stored.append(copy)
    for copy in stored:
        copy.wait()


def down(hidden, down_weight, me, expert, capacity, outputs):
    groups = len(hidden)
    count, units = hidden[0].shape
    experts, share = down_weight.shape[0], down_weight.shape[2]
    anywhere = pl.BlockSpec(memory_space=pl.ANY)
    vmem = pl.BlockSpec(memory_space=pltpu.VMEM)
    held = [] if outputs is None else [outputs]
    return pl.pallas_call(
        functools.partial(down_kernel, groups, expert),
        in_specs=[pl.BlockSpec(memory_space=pltpu.SMEM)]
        + [vmem] * (groups + 1)
        + [anywhere] * len(held),
        out_specs=anywhere,
        out_shape=jax.ShapeDtypeStruct(
            (count // (groups * capacity), groups, experts, capacity, share), jnp.bfloat16
        ),
        scratch_shapes=[
            pltpu.VMEM((count // capacity, capacity, share), jnp.bfloat16),
            pltpu.SemaphoreType.DMA((groups,)),
        ],
        input_output_aliases={groups + 2: 0} if held else {},
        compiler_params=pltpu.CompilerParams(vmem_limit_bytes=VMEM_LIMIT),
        cost_estimate=pl.CostEstimate(flops=1000, bytes_accessed=1000, transcendentals=0),
        name="down",
    )(me, *(in_vmem(x) for x in (*hidden, down_weight)), *held)


def combine_kernel(groups, combiner_ref, back_ref, mixed_ref):
    share = back_ref.shape[4]
    for g in range(groups):
        rows = back_ref[:, g]
        rows = rows.reshape((-1,) + rows.shape[2:]).reshape(-1, share)
        mixed_ref[:, g * share : (g + 1) * share] = jnp.dot(
            combiner_ref[...], rows, preferred_element_type=jnp.float32
        ).astype(mixed_ref.dtype)


def combine(combiner, back, groups):
    vmem = pl.BlockSpec(memory_space=pltpu.VMEM)
    return pl.pallas_call(
        functools.partial(combine_kernel, groups),
        in_specs=[vmem, vmem],
        out_shape=jax.ShapeDtypeStruct((combiner.shape[0], groups * back.shape[4]), jnp.bfloat16),
        compiler_params=pltpu.CompilerParams(vmem_limit_bytes=VMEM_LIMIT),
        cost_estimate=pl.CostEstimate(flops=1000, bytes_accessed=1000, transcendentals=0),
        name="combine",
    )(combiner, in_vmem(back))


def relayout_kernel(x_ref, *refs):
    refs[-1][...] = x_ref[...].reshape(refs[-1].shape)


def relayout(x, shape, after):
    return pl.pallas_call(
        relayout_kernel,
        in_specs=[pl.BlockSpec(memory_space=pltpu.VMEM)]
        + [pl.BlockSpec(memory_space=pl.ANY)] * len(after),
        out_shape=jax.ShapeDtypeStruct(shape, x.dtype),
        compiler_params=pltpu.CompilerParams(vmem_limit_bytes=VMEM_LIMIT),
        cost_estimate=pl.CostEstimate(flops=1000, bytes_accessed=1000, transcendentals=0),
        name="relayout",
    )(x, *after)


def pack_kernel(routing_ref, tokens_ref, down_ref, mask_ref, out_ref):
    tokens = tokens_ref[...]
    low = jnp.dot(tokens, down_ref[...], preferred_element_type=jnp.float32) * mask_ref[...]
    width = tokens.shape[1]
    share = width // 4
    for c in range(4):
        here = slice(c * share, (c + 1) * share)
        picked = jnp.dot(routing_ref[...], tokens[:, here], preferred_element_type=jnp.float32)
        out_ref[:, :, here] = picked.astype(out_ref.dtype).reshape(out_ref.shape[:2] + (share,))
    picked = jnp.dot(
        routing_ref[...], low.astype(out_ref.dtype), preferred_element_type=jnp.float32
    )
    out_ref[:, :, width:] = picked.astype(out_ref.dtype).reshape(
        out_ref.shape[:2] + (low.shape[1],)
    )


def pack(routing, tokens, adapter_down_factor, mask, owners):
    slots, adapters = routing.shape[0], mask.shape[1]
    vmem = pl.BlockSpec(memory_space=pltpu.VMEM)
    return pl.pallas_call(
        pack_kernel,
        in_specs=[vmem] * 4,
        out_shape=jax.ShapeDtypeStruct(
            (owners, slots // owners, tokens.shape[1] + adapters), jnp.bfloat16
        ),
        compiler_params=pltpu.CompilerParams(vmem_limit_bytes=VMEM_LIMIT),
        cost_estimate=pl.CostEstimate(flops=1000, bytes_accessed=1000, transcendentals=0),
        name="pack",
    )(routing, in_hbm(tokens), in_hbm(adapter_down_factor), mask)


def from_further(x, by):
    n = lax.axis_size("rep")
    return lax.ppermute(x, "rep", [(i, (i - by) % n) for i in range(n)])


def per_device(
    tokens,
    chosen_expert_index,
    expert_mixing_weight,
    row_adapter_index,
    gate_weight,
    up_weight,
    down_weight,
    adapter_down_factor,
    adapter_up_factor,
):
    row_count, width = tokens.shape
    owners = lax.axis_size("ep")
    groups = lax.axis_size("rep")
    local_count = gate_weight.shape[0]
    experts = local_count * owners
    capacity = 2
    share = down_weight.shape[2]
    f32 = jnp.float32
    bf16 = jnp.bfloat16

    flat_ids = chosen_expert_index.reshape(-1)
    one_hot = (flat_ids[:, None] == lax.iota(jnp.int32, experts)[None, :]).astype(jnp.int32)
    before = jnp.cumsum(one_hot, axis=0) - one_hot
    position = jnp.sum(before * one_hot, axis=1).reshape(chosen_expert_index.shape)
    local = chosen_expert_index % local_count
    owner = chosen_expert_index // local_count

    adapters = adapter_down_factor.shape[1]
    lane_adapter = lax.iota(jnp.int32, adapters) // ADAPTER_RANK
    adapter_mask = (row_adapter_index[:, None] == lane_adapter[None, :]).astype(f32)
    slots = owners * capacity
    slot = owner * capacity + position
    mixing = expert_mixing_weight.astype(f32)
    received, combiners = [], []
    for j in range(local_count):
        matches = (slot[:, :, None] == lax.iota(jnp.int32, slots)[None, None, :]) & (
            local == j
        )[:, :, None]
        routing = (
            (slot[None, :, :] == lax.iota(jnp.int32, slots)[:, None, None])
            & (local == j)[None, :, :]
        )
        routing = jnp.any(routing, axis=2).astype(bf16)
        combiners.append(
            jnp.sum(jnp.where(matches, mixing[:, :, None], f32(0.0)), axis=1).astype(bf16)
        )
        packed = pack(
            routing, tokens, adapter_down_factor, adapter_mask, owners
        )
        sent = lax.all_to_all(packed, "ep", split_axis=0, concat_axis=0, tiled=True)
        received.append(sent)

    me = lax.axis_index("rep").astype(jnp.int32).reshape(1)
    half = slots // 2
    back = None
    for j, sent in enumerate(received):
        mine = relayout(sent, (slots, width + adapters), [])
        before_me, after_me = from_further(mine, -1), from_further(mine, 1)
        across = [from_further(before_me[:half], -1), from_further(after_me[half:], 1)]
        every = [mine, after_me, *across, before_me]
        units = gate_up(every, gate_weight, up_weight, adapter_up_factor, j)
        hidden = [units] + [from_further(units, s) for s in range(1, groups)]
        back = down(hidden, down_weight, me, j, capacity, back)
    shape = back.shape
    back = back.reshape((owners * groups,) + shape[2:])
    back = lax.all_to_all(back, ("ep", "rep"), split_axis=0, concat_axis=0, tiled=True)
    back = back.reshape(shape)
    combiner = jnp.stack([c.reshape(row_count, owners, capacity) for c in combiners], axis=2)
    return combine(combiner.reshape(row_count, -1), back, groups)


def solution(mesh):
    placed = (
        P(("rep", "ep"), None),
        P(("rep", "ep"), None),
        P(("rep", "ep"), None),
        P(("rep", "ep")),
        P("ep", None, "rep"),
        P("ep", None, "rep"),
        P("ep", None, "rep"),
        P(),
        P(None, "rep"),
    )
    return jax.shard_map(
        per_device, mesh=mesh, in_specs=placed, out_specs=P(("rep", "ep"), None), check_vma=False
    )
```

```python
import functools

import jax
import jax.numpy as jnp
from jax import lax
from jax.experimental import pallas as pl
from jax.experimental.pallas import tpu as pltpu
from jax.sharding import PartitionSpec as P

ADAPTER_RANK = 16
VMEM_LIMIT = 16 * 1024 * 1024


def in_vmem(x):
    return pltpu.with_memory_space_constraint(x, pltpu.VMEM)


def in_hbm(x):
    return pltpu.with_memory_space_constraint(x, pltpu.HBM)


def gate_up_kernel(parts, expert, chunks, *refs):
    rows = refs[:parts]
    gate_ref, up_ref, factor_ref, hidden_ref, up_at, sem = refs[parts:]
    fetch = pltpu.make_async_copy(up_ref.at[expert], up_at, sem)
    fetch.start()
    width = gate_ref.shape[1]
    depth = width // chunks
    low = jnp.concatenate([r[:, width:] for r in rows], axis=0)
    up = jnp.dot(low, factor_ref[...], preferred_element_type=jnp.float32)
    gate = 0.0
    for c in range(chunks):
        here = slice(c * depth, (c + 1) * depth)
        x = jnp.concatenate([r[:, here] for r in rows], axis=0)
        gate += jnp.dot(x, gate_ref[expert, here], preferred_element_type=jnp.float32)
    fetch.wait()
    for c in range(chunks):
        here = slice(c * depth, (c + 1) * depth)
        x = jnp.concatenate([r[:, here] for r in rows], axis=0)
        up += jnp.dot(x, up_at[here], preferred_element_type=jnp.float32)
    hidden_ref[...] = (gate / (1.0 + jnp.exp(-gate)) * up).astype(hidden_ref.dtype)


def gate_up(rows, gate_weight, up_weight, factor, expert, chunks=7):
    units = gate_weight.shape[2]
    parts = len(rows)
    count = sum(r.shape[0] for r in rows)
    vmem = pl.BlockSpec(memory_space=pltpu.VMEM)
    return pl.pallas_call(
        functools.partial(gate_up_kernel, parts, expert, chunks),
        in_specs=[vmem] * (parts + 1) + [pl.BlockSpec(memory_space=pl.ANY), vmem],
        out_specs=vmem,
        out_shape=jax.ShapeDtypeStruct((count, units), jnp.bfloat16),
        scratch_shapes=[
            pltpu.VMEM(up_weight.shape[1:], jnp.bfloat16),
            pltpu.SemaphoreType.DMA,
        ],
        compiler_params=pltpu.CompilerParams(vmem_limit_bytes=VMEM_LIMIT),
        cost_estimate=pl.CostEstimate(flops=1000, bytes_accessed=1000, transcendentals=0),
        name="gate_up",
    )(*(in_vmem(x) for x in (*rows, gate_weight)), in_hbm(up_weight), factor)


def down_kernel(groups, expert, me_ref, *refs):
    hidden, weight_ref = refs[:groups], refs[groups]
    out_ref, made, sems = refs[-3:]
    count, units = hidden[0].shape
    block = count // groups
    me = me_ref[0]
    weights, columns = [], []
    for s in range(groups):
        at = pl.multiple_of(lax.rem(me + s, groups) * units, units)
        weights.append(weight_ref[expert, pl.ds(at, units)])
        turned = [(i - s) % groups * block for i in range(groups)]
        columns.append(jnp.concatenate([hidden[s][t : t + block] for t in turned], axis=0))
    out = jnp.dot(
        jnp.concatenate(columns, axis=1),
        jnp.concatenate(weights, axis=0),
        preferred_element_type=jnp.float32,
    )
    out = out.astype(made.dtype)
    stored = []
    for i in range(groups):
        senders = block // made.shape[1]
        made[i * senders : (i + 1) * senders] = out[i * block : (i + 1) * block].reshape(
            (senders,) + made.shape[1:]
        )
        to = pl.ds(lax.rem(me + i, groups) * senders, senders)
        copy = pltpu.make_async_copy(
            made.at[pl.ds(i * senders, senders)], out_ref.at[to, expert], sems.at[i]
        )
        copy.start()
        stored.append(copy)
    for copy in stored:
        copy.wait()


def down(hidden, down_weight, me, expert, capacity, outputs):
    groups = len(hidden)
    count, units = hidden[0].shape
    experts, share = down_weight.shape[0], down_weight.shape[2]
    anywhere = pl.BlockSpec(memory_space=pl.ANY)
    vmem = pl.BlockSpec(memory_space=pltpu.VMEM)
    held = [] if outputs is None else [outputs]
    return pl.pallas_call(
        functools.partial(down_kernel, groups, expert),
        in_specs=[pl.BlockSpec(memory_space=pltpu.SMEM)]
        + [vmem] * (groups + 1)
        + [anywhere] * len(held),
        out_specs=anywhere,
        out_shape=jax.ShapeDtypeStruct((count // capacity, experts, capacity, share), jnp.bfloat16),
        scratch_shapes=[
            pltpu.VMEM((count // capacity, capacity, share), jnp.bfloat16),
            pltpu.SemaphoreType.DMA((groups,)),
        ],
        input_output_aliases={groups + 2: 0} if held else {},
        compiler_params=pltpu.CompilerParams(vmem_limit_bytes=VMEM_LIMIT),
        cost_estimate=pl.CostEstimate(flops=1000, bytes_accessed=1000, transcendentals=0),
        name="down",
    )(me, *(in_vmem(x) for x in (*hidden, down_weight)), *held)


def combine_kernel(groups, combiner_ref, back_ref, mixed_ref):
    senders = back_ref.shape[0] // groups
    share = back_ref.shape[3]
    for g in range(groups):
        rows = back_ref[g * senders : (g + 1) * senders]
        rows = rows.reshape((-1,) + rows.shape[2:]).reshape(-1, share)
        mixed_ref[:, g * share : (g + 1) * share] = jnp.dot(
            combiner_ref[...], rows, preferred_element_type=jnp.float32
        ).astype(mixed_ref.dtype)


def combine(combiner, back, groups):
    vmem = pl.BlockSpec(memory_space=pltpu.VMEM)
    return pl.pallas_call(
        functools.partial(combine_kernel, groups),
        in_specs=[vmem, vmem],
        out_shape=jax.ShapeDtypeStruct((combiner.shape[0], groups * back.shape[3]), jnp.bfloat16),
        compiler_params=pltpu.CompilerParams(vmem_limit_bytes=VMEM_LIMIT),
        cost_estimate=pl.CostEstimate(flops=1000, bytes_accessed=1000, transcendentals=0),
        name="combine",
    )(combiner, in_vmem(back))


def relayout_kernel(x_ref, *refs):
    refs[-1][...] = x_ref[...].reshape(refs[-1].shape)


def relayout(x, shape, after):
    return pl.pallas_call(
        relayout_kernel,
        in_specs=[pl.BlockSpec(memory_space=pltpu.VMEM)]
        + [pl.BlockSpec(memory_space=pl.ANY)] * len(after),
        out_shape=jax.ShapeDtypeStruct(shape, x.dtype),
        compiler_params=pltpu.CompilerParams(vmem_limit_bytes=VMEM_LIMIT),
        cost_estimate=pl.CostEstimate(flops=1000, bytes_accessed=1000, transcendentals=0),
        name="relayout",
    )(x, *after)


def halves_kernel(half, before_ref, after_ref, *refs):
    top_ref, bottom_ref = refs[-2:]
    top_ref[...] = before_ref[:half]
    bottom_ref[...] = after_ref[half:]


def halves(before_me, after_me, after):
    count, width = before_me.shape
    half = count // 2
    vmem = pl.BlockSpec(memory_space=pltpu.VMEM)
    return pl.pallas_call(
        functools.partial(halves_kernel, half),
        in_specs=[vmem, vmem] + [pl.BlockSpec(memory_space=pl.ANY)] * len(after),
        out_shape=[jax.ShapeDtypeStruct((half, width), before_me.dtype)] * 2,
        compiler_params=pltpu.CompilerParams(vmem_limit_bytes=VMEM_LIMIT),
        cost_estimate=pl.CostEstimate(flops=1000, bytes_accessed=1000, transcendentals=0),
        name="halves",
    )(before_me, after_me, *after)


def pack_kernel(routing_ref, tokens_ref, down_ref, mask_ref, out_ref):
    tokens = tokens_ref[...]
    low = jnp.dot(tokens, down_ref[...], preferred_element_type=jnp.float32) * mask_ref[...]
    width = tokens.shape[1]
    share = width // 4
    for c in range(4):
        here = slice(c * share, (c + 1) * share)
        picked = jnp.dot(routing_ref[...], tokens[:, here], preferred_element_type=jnp.float32)
        out_ref[:, :, here] = picked.astype(out_ref.dtype).reshape(out_ref.shape[:2] + (share,))
    picked = jnp.dot(
        routing_ref[...], low.astype(out_ref.dtype), preferred_element_type=jnp.float32
    )
    out_ref[:, :, width:] = picked.astype(out_ref.dtype).reshape(
        out_ref.shape[:2] + (low.shape[1],)
    )


def pack(routing, tokens, adapter_down_factor, mask, owners):
    slots, adapters = routing.shape[0], mask.shape[1]
    vmem = pl.BlockSpec(memory_space=pltpu.VMEM)
    return pl.pallas_call(
        pack_kernel,
        in_specs=[vmem] * 4,
        out_shape=jax.ShapeDtypeStruct(
            (owners, slots // owners, tokens.shape[1] + adapters), jnp.bfloat16
        ),
        compiler_params=pltpu.CompilerParams(vmem_limit_bytes=VMEM_LIMIT),
        cost_estimate=pl.CostEstimate(flops=1000, bytes_accessed=1000, transcendentals=0),
        name="pack",
    )(routing, in_hbm(tokens), in_hbm(adapter_down_factor), mask)


def from_further(x, by):
    n = lax.axis_size("rep")
    return lax.ppermute(x, "rep", [(i, (i - by) % n) for i in range(n)])


def per_device(
    tokens,
    chosen_expert_index,
    expert_mixing_weight,
    row_adapter_index,
    gate_weight,
    up_weight,
    down_weight,
    adapter_down_factor,
    adapter_up_factor,
):
    row_count, width = tokens.shape
    owners = lax.axis_size("ep")
    groups = lax.axis_size("rep")
    local_count = gate_weight.shape[0]
    experts = local_count * owners
    capacity = 2
    share = down_weight.shape[2]
    f32 = jnp.float32
    bf16 = jnp.bfloat16

    flat_ids = chosen_expert_index.reshape(-1)
    one_hot = (flat_ids[:, None] == lax.iota(jnp.int32, experts)[None, :]).astype(jnp.int32)
    before = jnp.cumsum(one_hot, axis=0) - one_hot
    position = jnp.sum(before * one_hot, axis=1).reshape(chosen_expert_index.shape)
    local = chosen_expert_index % local_count
    owner = chosen_expert_index // local_count

    adapters = adapter_down_factor.shape[1]
    lane_adapter = lax.iota(jnp.int32, adapters) // ADAPTER_RANK
    adapter_mask = (row_adapter_index[:, None] == lane_adapter[None, :]).astype(f32)
    slots = owners * capacity
    slot = owner * capacity + position
    mixing = expert_mixing_weight.astype(f32)
    received, combiners = [], []
    for j in range(local_count):
        matches = (slot[:, :, None] == lax.iota(jnp.int32, slots)[None, None, :]) & (
            local == j
        )[:, :, None]
        routing = (
            (slot[None, :, :] == lax.iota(jnp.int32, slots)[:, None, None])
            & (local == j)[None, :, :]
        )
        routing = jnp.any(routing, axis=2).astype(bf16)
        combiners.append(
            jnp.sum(jnp.where(matches, mixing[:, :, None], f32(0.0)), axis=1).astype(bf16)
        )
        packed = pack(
            routing, tokens, adapter_down_factor, adapter_mask, owners
        )
        sent = lax.all_to_all(packed, "ep", split_axis=0, concat_axis=0, tiled=True)
        received.append(sent)

    me = lax.axis_index("rep").astype(jnp.int32).reshape(1)
    half = slots // 2
    back = None
    for j, sent in enumerate(received):
        mine = relayout(sent, (slots, width + adapters), [])
        before_me, after_me = from_further(mine, -1), from_further(mine, 1)
        across = [from_further(before_me[:half], -1), from_further(after_me[half:], 1)]
        every = [mine, after_me, *across, before_me]
        units = gate_up(every, gate_weight, up_weight, adapter_up_factor, j)
        hidden = [units] + [from_further(units, s) for s in range(1, groups)]
        back = down(hidden, down_weight, me, j, capacity, back)
    back = lax.all_to_all(back, ("rep", "ep"), split_axis=0, concat_axis=0, tiled=True)
    combiner = jnp.stack([c.reshape(row_count, owners, capacity) for c in combiners], axis=2)
    return combine(combiner.reshape(row_count, -1), back, groups)


def solution(mesh):
    placed = (
        P(("rep", "ep"), None),
        P(("rep", "ep"), None),
        P(("rep", "ep"), None),
        P(("rep", "ep")),
        P("ep", None, "rep"),
        P("ep", None, "rep"),
        P("ep", None, "rep"),
        P(),
        P(None, "rep"),
    )
    return jax.shard_map(
        per_device, mesh=mesh, in_specs=placed, out_specs=P(("rep", "ep"), None), check_vma=False
    )
```
